1024 devices in a mesh: dp: 64 (over z, y_lo, core), tensor: 16 (over x, y_hi).
Axes of the slice: x: 8, y: 8 (y_hi: 2, y_lo: 4; y = y_hi * 4 + y_lo), z: 8, core: 2. Of those that a mesh axis runs over, the one named last changes fastest.
Arguments:
- tokens: bfloat16 [16384, 8192], P('dp', 'tensor'), may hold values from -6 to 6
- weight: bfloat16 [1024, 8192], P('dp', 'tensor'), may hold values from -0.0625 to 0.0625
- cotangent: bfloat16 [16384, 1024], P(('dp', 'tensor')), may hold values from -24 to 24
Outputs:
- outputs: bfloat16 [16384, 1024], P(('dp', 'tensor'))
- grad_tokens: bfloat16 [16384, 8192], P('dp', 'tensor')
- weight_grad: float32 [1024, 8192], P('dp', 'tensor')
The draws below stay inside these ranges and needn't reach their ends.
All inputs are finite; a program needn't handle non-finite values.
Results may differ from the reference program's by a relative error of at most 0.019.
Values may be sent and summed in bfloat16 or wider, within the bound.
A program may use at most 32 MiB of HBM per device.

```python
import jax
import jax.numpy as jnp
from jax import lax

D = 8192
KV = 1024
TOKENS = 16384
N_TENSOR = 16


def spiked(result, key, source, target, blocks, factor):
    owner, partner = [(jnp.arange(result.shape[position]) // (result.shape[position] // blocks)).reshape([-1 if axis == position else 1 for axis in range(result.ndim)]) for position in (source, target)]
    chosen = jax.random.permutation(key, blocks)[partner]
    strong = (owner == chosen) | (owner == (partner + blocks // 2) % blocks)
    return jnp.where(strong, factor * result, result)


def shard_levels(own_key, shape, split, smallest, high):
    gain, own = 1.0, jax.random.fold_in(own_key, 6)
    for axis_at, blocks in split:
        draws = jnp.exp(jax.random.uniform(jax.random.fold_in(own, axis_at), (blocks,), jnp.float32, smallest / len(split), high / len(split)))
        gain = gain * jnp.repeat(draws, shape[axis_at] // blocks).reshape([-1 if axis == axis_at else 1 for axis in range(len(shape))])
    return gain


def noise(key, extent, deviation, bound, pieces=(), held_as=jnp.bfloat16):
    factor_of = shard_levels(key, extent, pieces, -0.22, 0.18) if pieces else 1.0
    array = jax.random.normal(key, extent, jnp.float32) * deviation * factor_of
    return jnp.minimum(jnp.maximum(array, -bound), bound).astype(held_as)


def heavy_noise(own_key, shape, spread, bound, shards, heavy, held_as=jnp.bfloat16):
    drawn = spread * jax.random.normal(own_key, shape, jnp.float32)
    if shards:
        drawn = drawn * shard_levels(own_key, shape, shards, -0.22, 0.18)
    return jnp.clip(spiked(drawn, jax.random.fold_in(own_key, 3), *heavy), -bound, bound).astype(held_as)


def setup_inputs(seed: int = 0) -> dict:
    seeds = jax.random.split(jax.random.key(seed), 4)
    return {
        "tokens": noise(seeds[0], (TOKENS, D), 1.0, 6.0, ((0, 64), (1, 16))),
        "weight": noise(seeds[1], (KV, D), D ** -0.5, 0.0625, ((0, 64), (1, 16))),
        "cotangent": heavy_noise(seeds[2], (TOKENS, KV), 1.0, 24.0, ((0, 1024),), (0, 1, 1024, 6.0)),
    }


def signs_table(order_size):
    bit_count = order_size.bit_length() - 1
    positions = lax.iota(jnp.int32, order_size)
    parity = jnp.zeros((order_size, order_size), jnp.int32)
    for bit_number in range(bit_count):
        parity = parity + ((positions[:, None] >> bit_number) & 1) * ((positions[None, :] >> bit_number) & 1)
    return (1 - 2 * (parity % 2)).astype(jnp.bfloat16)


def pair_section(values, section_number):
    row_count, blocks, width = values.shape
    half_span = 2 ** section_number
    grouped = values.reshape(row_count, blocks // (2 * half_span), 2, half_span, width).astype(jnp.float32)
    lower_half = grouped[:, :, 0]
    upper_half = grouped[:, :, 1]
    joined = jnp.stack([lower_half + upper_half, lower_half - upper_half], axis=2) * jnp.float32(0.5 ** 0.5)
    return joined.reshape(row_count, blocks, width).astype(jnp.bfloat16)


def rotate(values):
    row_count = values.shape[0]
    width = D // N_TENSOR
    blended = jnp.dot(values.reshape(row_count * N_TENSOR, width), signs_table(width), preferred_element_type=jnp.float32)
    blended = (blended * jnp.float32(width ** -0.5)).astype(jnp.bfloat16).reshape(row_count, N_TENSOR, width)
    for section_number in range(N_TENSOR.bit_length() - 1):
        blended = pair_section(blended, section_number)
    return blended.reshape(row_count, D)


def reference(tokens, weight, cotangent):
    width = D // N_TENSOR
    rotated = rotate(tokens)
    running = jnp.zeros((TOKENS, KV), jnp.float32)
    for block_no in range(N_TENSOR):
        partial_value = jnp.dot(rotated[:, block_no * width:(block_no + 1) * width], weight[:, block_no * width:(block_no + 1) * width].T, preferred_element_type=jnp.float32).astype(jnp.bfloat16)
        partial_value = lax.optimization_barrier(partial_value)
        running = running + partial_value.astype(jnp.float32)
    outputs = running.astype(jnp.bfloat16)
    grad_rotated = jnp.dot(cotangent, weight, preferred_element_type=jnp.float32).astype(jnp.bfloat16)
    grad_tokens = rotate(grad_rotated)
    weight_grad = jnp.dot(cotangent.T, rotated, preferred_element_type=jnp.float32) * jnp.float32(TOKENS ** -0.5)
    return (outputs, grad_tokens, weight_grad)
```

```python
import functools

import jax
import jax.numpy as jnp
from jax import lax
from jax.experimental import pallas as pl
from jax.experimental.pallas import tpu as pltpu
from jax.sharding import PartitionSpec as P

Z, YL, NC = 8, 4, 2
X, YH = 8, 2
K = 16
INTERPRET = False
F32, BF16 = jnp.float32, jnp.bfloat16


def signs_table(width):
    bits = lax.broadcasted_iota(jnp.int32, (width, width), 0) & lax.broadcasted_iota(
        jnp.int32, (width, width), 1
    )
    for shift in (8, 4, 2, 1):
        bits = bits ^ (bits >> shift)
    return (1 - 2 * (bits & 1)).astype(F32).astype(BF16)


def sign(a, b):
    bits = a & b
    bits = bits ^ (bits >> 2)
    bits = bits ^ (bits >> 1)
    return (1 - 2 * (bits & 1)).astype(F32)


def kernel(
    norm,
    tok, wgt, cot,
    out, gtok, gwgt,
    tbuf, trot, signs, wx, wy, wall, call, pbuf, pcore, psum, prz, py, pry, px,
    obuf, orx, oy, ory, obuf_out, gbuf, gwbuf,
    lsem, wx_s, wx_r, wy_s, wy_r, wz_s, wz_r, wc_s, wc_r, cy_s, cy_r, ca_s, ca_r, cb_s, cb_r,
    pc_s, pc_r, pz_s, pz_r, py_s, py_r, px_s, px_r, ox_s, ox_r, oy_s, oy_r,
):
    width = tbuf.shape[1]
    kv = cot.shape[1]
    group = YL * NC * K
    d, t = lax.axis_index("dp"), lax.axis_index("tensor")
    z, yl, c = d // (YL * NC), (d // NC) % YL, d % NC
    x, yh = t // YH, t % YH
    yy = yh * YL + yl
    NY = YL * YH

    def at_x(r):
        return {"dp": d, "tensor": ((x + r) % X) * YH + yh}

    def at_z(r):
        return {"dp": (((z + r) % Z) * YL + yl) * NC + c, "tensor": t}

    def at_y(r):
        v = (yy + r) % NY
        return {"dp": (z * YL + v % YL) * NC + c, "tensor": x * YH + v // YL}

    at_core = {"dp": (z * YL + yl) * NC + (1 - c), "tensor": t}

    def remote(src, dst, s, r, where):
        return pltpu.make_async_remote_copy(
            src_ref=src, dst_ref=dst, send_sem=s, recv_sem=r,
            device_id=where, device_id_type=pl.DeviceIdType.MESH,
        )

    sends = []

    def send(src, dst, s, r, where):
        copy = remote(src, dst, s, r, where)
        copy.start()
        sends.append(copy)

    def wait_in(dst, s, r):
        remote(dst, dst, s, r, at_core).wait_recv()

    load_w = pltpu.make_async_copy(wgt, wx.at[0], lsem.at[0])
    load_c = pltpu.make_async_copy(cot, call.at[x, yh], lsem.at[1])
    load_t = pltpu.make_async_copy(tok, tbuf, lsem.at[2])
    load_w.start()
    load_c.start()
    load_t.start()

    peers = (
        [at_x(r) for r in range(1, X)]
        + [at_y(r) for r in range(1, NY)]
        + [at_z(r) for r in range(1, Z)]
        + [at_core]
    )
    barrier = pltpu.get_barrier_semaphore()
    for peer in peers:
        pl.semaphore_signal(barrier, inc=1, device_id=peer, device_id_type=pl.DeviceIdType.MESH)
    signs[...] = signs_table(width)
    load_w.wait()
    load_c.wait()
    pl.semaphore_wait(barrier, len(peers))

    for r in range(1, X):
        send(wx.at[0], wx.at[r], wx_s.at[r], wx_r.at[r], at_x(r))
    send(call.at[x, yh], call.at[x, yh], cy_s.at[0], cy_r.at[0], at_y(YL))
    for r in range(1, X):
        send(call.at[x, yh], call.at[x, yh], ca_s.at[r], ca_r.at[r], at_x(r))

    load_t.wait()
    root = F32(width ** -0.5)
    trot[...] = (jnp.dot(tbuf[...], signs[...], preferred_element_type=F32) * root).astype(BF16)

    for r in range(1, X):
        wait_in(wx.at[r], wx_s.at[r], wx_r.at[r])
    mixed = wx[0].astype(F32) * sign(x, x)
    for r in range(1, X):
        mixed = mixed + wx[r].astype(F32) * sign(x, (x + X - r) % X)
    wy[0] = (mixed * F32(X ** -0.5)).astype(BF16)
    for r in range(1, NY):
        send(wy.at[0], wy.at[r], wy_s.at[r], wy_r.at[r], at_y(r))

    wait_in(call.at[x, 1 - yh], cy_s.at[0], cy_r.at[0])
    for r in range(1, X):
        send(call.at[x, 1 - yh], call.at[x, 1 - yh], cb_s.at[r], cb_r.at[r], at_x(r))

    for r in range(1, NY):
        wait_in(wy.at[r], wy_s.at[r], wy_r.at[r])
    for r in range(YL):
        pair = wy[r].astype(F32) * sign(yh, ((yy + NY - r) % NY) // YL)
        pair = pair + wy[r + YL].astype(F32) * sign(yh, ((yy + NY - r - YL) % NY) // YL)
        wall[z, (yl + YL - r) % YL, c] = (pair * F32(0.5 ** 0.5)).astype(BF16)
    for r in range(1, Z):
        send(wall.at[z, :, c], wall.at[z, :, c], wz_s.at[r], wz_r.at[r], at_z(r))
    send(wall.at[z, :, c], wall.at[z, :, c], wc_s.at[0], wc_r.at[0], at_core)

    for r in range(1, X):
        src = (x + X - r) % X
        wait_in(call.at[src, yh], ca_s.at[r], ca_r.at[r])
        wait_in(call.at[src, 1 - yh], cb_s.at[r], cb_r.at[r])
    for r in list(range(1, Z)) + [0]:
        zz = (z + r) % Z
        cols = call[:, :, :, pl.ds(pl.multiple_of(zz * group, group), group)]
        part = lax.dot_general(
            cols.reshape(X * YH * K, group), trot[...], (((0,), (0,)), ((), ())),
            preferred_element_type=F32,
        )
        pbuf[zz] = part.astype(BF16).reshape(YL, NC, K, width)
        send(pbuf.at[zz, :, 1 - c], pcore.at[zz], pc_s.at[r], pc_r.at[r], at_core)

    for r in range(1, Z):
        src = (z + Z - r) % Z
        wait_in(wall.at[src, :, c], wz_s.at[r], wz_r.at[r])
        send(wall.at[src, :, c], wall.at[src, :, c], wc_s.at[r], wc_r.at[r], at_core)

    for r in list(range(1, Z)) + [0]:
        zz = (z + r) % Z
        wait_in(pcore.at[zz], pc_s.at[r], pc_r.at[r])
        total = pbuf[zz, :, c].astype(F32) + pcore[zz].astype(F32)
        psum[zz] = total.astype(BF16)
        if r:
            send(psum.at[zz], prz.at[r], pz_s.at[r], pz_r.at[r], at_z(r))

    for r in range(Z):
        src = (z + Z - r) % Z
        wait_in(wall.at[src, :, 1 - c], wc_s.at[r], wc_r.at[r])
    for n in range(Z):
        part = lax.dot_general(
            trot[...], wall[n].reshape(group, width), (((1,), (1,)), ((), ())),
            preferred_element_type=F32,
        )
        obuf[:, :, :, n * group:(n + 1) * group] = part.astype(BF16).reshape(X, YH, K, group)
    for r in range(1, X):
        send(obuf.at[(x + r) % X], orx.at[r], ox_s.at[r], ox_r.at[r], at_x(r))

    half = X // 2
    for n in range(2):
        rows = call[n * half:(n + 1) * half].reshape(half * YH * K, kv)
        grad = jnp.dot(rows, wall[...].reshape(kv, width), preferred_element_type=F32)
        grad = jnp.dot(grad.astype(BF16), signs[...], preferred_element_type=F32) * root
        gbuf[n * half * YH * K:(n + 1) * half * YH * K] = grad.astype(BF16)
    store_g = pltpu.make_async_copy(gbuf, gtok, lsem.at[3])
    store_g.start()

    total = psum[z].astype(F32)
    for r in range(1, Z):
        wait_in(prz.at[r], pz_s.at[r], pz_r.at[r])
        total = total + prz[r].astype(F32)
    py[...] = total.astype(BF16)
    for r in range(1, NY):
        send(py.at[(yl + r) % YL], pry.at[r], py_s.at[r], py_r.at[r], at_y(r))

    total = obuf[x].astype(F32)
    for r in range(1, X):
        wait_in(orx.at[r], ox_s.at[r], ox_r.at[r])
        total = total + orx[r].astype(F32)
    oy[...] = total.astype(BF16)
    send(oy.at[1 - yh], ory, oy_s.at[0], oy_r.at[0], at_y(YL))

    total = py[yl].astype(F32) * sign(yh, yh)
    for r in range(1, NY):
        wait_in(pry.at[r], py_s.at[r], py_r.at[r])
        total = total + pry[r].astype(F32) * sign(yh, ((yy + NY - r) % NY) // YL)
    px[0] = total.astype(BF16)
    for r in range(1, X):
        send(px.at[0], px.at[r], px_s.at[r], px_r.at[r], at_x(r))

    wait_in(ory, oy_s.at[0], oy_r.at[0])
    obuf_out[...] = (oy[yh].astype(F32) + ory[...].astype(F32)).astype(BF16)
    store_o = pltpu.make_async_copy(obuf_out, out, lsem.at[4])
    store_o.start()

    total = px[0].astype(F32) * sign(x, x)
    for r in range(1, X):
        wait_in(px.at[r], px_s.at[r], px_r.at[r])
        total = total + px[r].astype(F32) * sign(x, (x + X - r) % X)
    gwbuf[...] = total * F32(norm * (X * YH) ** -0.5)
    store_w = pltpu.make_async_copy(gwbuf, gwgt, lsem.at[5])
    store_w.start()

    for copy in sends:
        copy.wait_send()
    store_g.wait()
    store_o.wait()
    store_w.wait()


def on_device(norm, tokens, weight, cotangent):
    rows, width = tokens.shape
    kv = cotangent.shape[1]
    vmem = pltpu.VMEM
    any_spec = pl.BlockSpec(memory_space=pl.ANY)
    dma = lambda n: pltpu.SemaphoreType.DMA((n,))
    scratch = [
        vmem((rows, width), BF16),
        vmem((rows, width), BF16),
        vmem((width, width), BF16),
        vmem((X, K, width), BF16),
        vmem((YL * YH, K, width), BF16),
        vmem((Z, YL, NC, K, width), BF16),
        vmem((X, YH, K, kv), BF16),
        vmem((Z, YL, NC, K, width), BF16),
        vmem((Z, YL, K, width), BF16),
        vmem((Z, YL, K, width), BF16),
        vmem((Z, YL, K, width), BF16),
        vmem((YL, K, width), BF16),
        vmem((YL * YH, K, width), BF16),
        vmem((X, K, width), BF16),
        vmem((X, YH, K, kv), BF16),
        vmem((X, YH, K, kv), BF16),
        vmem((YH, K, kv), BF16),
        vmem((K, kv), BF16),
        vmem((K, kv), BF16),
        vmem((rows, width), BF16),
        vmem((K, width), F32),
        dma(6),
    ]
    for n in (X, YL * YH, Z, Z, 1, X, X, Z, Z, YL * YH, X, X, 1):
        scratch += [dma(n), dma(n)]
    return pl.pallas_call(
        functools.partial(kernel, norm),
        out_shape=(
            jax.ShapeDtypeStruct((K, kv), BF16),
            jax.ShapeDtypeStruct((rows, width), BF16),
            jax.ShapeDtypeStruct((K, width), F32),
        ),
        in_specs=[any_spec] * 3,
        out_specs=(any_spec,) * 3,
        scratch_shapes=scratch,
        compiler_params=pltpu.CompilerParams(
            collective_id=0, has_side_effects=True, vmem_limit_bytes=40 * 2**20
        ),
    )(tokens, weight, cotangent)


def solution(mesh):
    assert dict(mesh.shape) == {"dp": Z * YL * NC, "tensor": X * YH}

    def whole(tokens, weight, cotangent):
        return jax.shard_map(
            functools.partial(on_device, tokens.shape[0] ** -0.5),
            mesh=mesh,
            in_specs=(P("dp", "tensor"), P("dp", "tensor"), P(("dp", "tensor"), None)),
            out_specs=(P(("dp", "tensor"), None), P("dp", "tensor"), P("dp", "tensor")),
            check_vma=False,
        )(tokens, weight, cotangent)

    return whole
```

```python
import functools

import jax
import jax.numpy as jnp
from jax import lax
from jax.experimental import pallas as pl
from jax.experimental.pallas import tpu as pltpu
from jax.sharding import PartitionSpec as P

Z, YL, NC = 8, 4, 2
X, YH = 8, 2
K = 16
WZD, PZD, CD, WF = True, False, True, False
WZD, PZD, ORD, CD, WF = True, True, 1, False, True
ZO = (4, 3, 5, 2, 6, 1, 7)
F32, BF16 = jnp.float32, jnp.bfloat16


def signs_table(width):
    bits = lax.broadcasted_iota(jnp.int32, (width, width), 0) & lax.broadcasted_iota(
        jnp.int32, (width, width), 1
    )
    for shift in (8, 4, 2, 1):
        bits = bits ^ (bits >> shift)
    return (1 - 2 * (bits & 1)).astype(F32).astype(BF16)


def sign(a, b):
    bits = a & b
    bits = bits ^ (bits >> 2)
    bits = bits ^ (bits >> 1)
    return (1 - 2 * (bits & 1)).astype(F32)


def kernel(
    norm,
    tok, wgt, cot,
    out, gtok, gwgt,
    tbuf, trot, signs, wx, wy, wall, call, pbuf, pcore, psum, prz, pnear, pfar, pmid, pfin, py, pry, px,
    obuf, onear, ofar, omid, ofin, oy, ory, obuf_out, gbuf, gwbuf,
    lsem, wx_s, wx_r, wy_s, wy_r, wz_s, wz_r, wf_s, wc_s, wc_r, cy_s, cy_r, ca_s, ca_r, cb_s, cb_r,
    pc_s, pc_r, pz_s, pz_r, py_s, py_r, px_s, px_r, ox_s, ox_r, oy_s, oy_r,
):
    width = tbuf.shape[1]
    group = YL * NC * K
    rows = X * YH * K
    d, t = lax.axis_index("dp"), lax.axis_index("tensor")
    z, yl, c = d // (YL * NC), (d // NC) % YL, d % NC
    x, yh = t // YH, t % YH
    yy = yh * YL + yl
    NY = YL * YH
    kv = cot.shape[1]

    def at_x(r):
        return {"dp": d, "tensor": ((x + r) % X) * YH + yh}

    def at_z(r):
        return {"dp": (((z + r) % Z) * YL + yl) * NC + c, "tensor": t}

    def at_y(r):
        v = (yy + r) % NY
        return {"dp": (z * YL + v % YL) * NC + c, "tensor": x * YH + v // YL}

    at_core = {"dp": (z * YL + yl) * NC + (1 - c), "tensor": t}

    def remote(src, dst, s, r, where):
        return pltpu.make_async_remote_copy(
            src_ref=src, dst_ref=dst, send_sem=s, recv_sem=r,
            device_id=where, device_id_type=pl.DeviceIdType.MESH,
        )

    sends = []

    def send(src, dst, s, r, where):
        copy = remote(src, dst, s, r, where)
        copy.start()
        sends.append(copy)

    def wait_in(dst, s, r):
        remote(dst, dst, s, r, at_core).wait_recv()

    load_w = pltpu.make_async_copy(wgt, wx.at[0], lsem.at[0])
    load_w.start()
    load_c = pltpu.make_async_copy(cot, call.at[x, yh], lsem.at[5])
    load_c.start()
    load_t = pltpu.make_async_copy(tok, tbuf, lsem.at[1])
    load_t.start()

    peers = (
        [at_x(r) for r in range(1, X)]
        + [at_y(r) for r in range(1, NY)]
        + [at_z(r) for r in range(1, Z)]
        + [at_core]
    )
    barrier = pltpu.get_barrier_semaphore()
    for peer in peers:
        pl.semaphore_signal(barrier, inc=1, device_id=peer, device_id_type=pl.DeviceIdType.MESH)
    signs[...] = signs_table(width)
    load_w.wait()
    load_c.wait()
    pl.semaphore_wait(barrier, len(peers))

    for r in range(1, X):
        send(wx.at[0], wx.at[r], wx_s.at[r], wx_r.at[r], at_x(r))
    own = call.at[x, yh]
    send(own, own, cy_s.at[0], cy_r.at[0], at_y(YL))
    near = (4, 3, 5, 2, 6, 1, 7) if CD else (2, X - 2, 1, X - 1)
    for r in near:
        send(own, own, ca_s.at[r], ca_r.at[r], at_x(r))

    load_t.wait()
    root = F32(width ** -0.5)
    trot[...] = (jnp.dot(tbuf[...], signs[...], preferred_element_type=F32) * root).astype(BF16)

    def pass_on(h, s, r, far):
        if CD:
            return
        for came, step in ((2, 1), (X - 2, X - 1)):
            piece = call.at[(x + X - came) % X, h]
            wait_in(piece, s.at[came], r.at[came])
            to = (came + step) % X
            send(piece, piece, s.at[to], r.at[to], at_x(step))
            if came == far:
                send(piece, piece, s.at[X // 2], r.at[X // 2], at_x(far))

    if not WF:
        pass_on(yh, ca_s, ca_r, 2)

    other = call.at[x, 1 - yh]
    wait_in(other, cy_s.at[0], cy_r.at[0])
    for r in near:
        send(other, other, cb_s.at[r], cb_r.at[r], at_x(r))

    for r in range(1, X):
        wait_in(wx.at[r], wx_s.at[r], wx_r.at[r])
    mixed = wx[0].astype(F32) * sign(x, x)
    for r in range(1, X):
        mixed = mixed + wx[r].astype(F32) * sign(x, (x + X - r) % X)
    wy[0] = (mixed * F32(X ** -0.5)).astype(BF16)
    for r in range(1, NY):
        send(wy.at[0], wy.at[r], wy_s.at[r], wy_r.at[r], at_y(r))

    if WF:
        pass_on(yh, ca_s, ca_r, 2)
    pass_on(1 - yh, cb_s, cb_r, X - 2)

    for r in range(1, NY):
        wait_in(wy.at[r], wy_s.at[r], wy_r.at[r])
    for r in range(YL):
        pair = wy[r].astype(F32) * sign(yh, ((yy + NY - r) % NY) // YL)
        pair = pair + wy[r + YL].astype(F32) * sign(yh, ((yy + NY - r - YL) % NY) // YL)
        wall[z, (yl + YL - r) % YL, c] = (pair * F32(0.5 ** 0.5)).astype(BF16)
    mine = wall.at[z, :, c]
    for r in (ZO if WZD else (2, Z - 2, 1, Z - 1)):
        send(mine, mine, wz_s.at[r], wz_r.at[r], at_z(r))
    remote(mine, mine, wc_s.at[z], wc_r.at[z], at_core).start()

    mid = YL // 2

    def pass_up(n):
        piece, part = wall.at[n, :, c], wall.at[n, pl.ds(0, mid), c]
        remote(piece, piece, wf_s.at[0], wz_r.at[3], at_z(1)).start()
        remote(part, part, wf_s.at[1], wz_r.at[4], at_z(2)).start()

    def pass_down(n):
        piece, part = wall.at[n, :, c], wall.at[n, pl.ds(mid, mid), c]
        remote(piece, piece, wf_s.at[2], wz_r.at[5], at_z(Z - 1)).start()
        remote(part, part, wf_s.at[3], wz_r.at[0], at_z(Z - 2)).start()

    @(lambda f: None if WZD else pl.when((z >= 2))(f))
    def _():
        n = (z + Z - 2) % Z
        wait_in(wall.at[n, :, c], wz_s.at[2], wz_r.at[2])
        pass_up(n)

    @(lambda f: None if WZD else pl.when((z >= Z - 2))(f))
    def _():
        n = (z + 2) % Z
        wait_in(wall.at[n, :, c], wz_s.at[Z - 2], wz_r.at[Z - 2])
        pass_down(n)

    for r in (range(1, X) if CD else (1, 3, 4, 5, 7)):
        src = (x + X - r) % X
        wait_in(call.at[src, yh], ca_s.at[r], ca_r.at[r])
        wait_in(call.at[src, 1 - yh], cb_s.at[r], cb_r.at[r])
    order = (3, 5, 4, 1, 7, 2, 6, 0)
    for r in order:
        first = pl.multiple_of(((z + r) % Z) * group, group)
        part = lax.dot_general(
            call[:, :, :, pl.ds(first, group)].reshape(rows, group), trot[...],
            (((0,), (0,)), ((), ())), preferred_element_type=F32,
        )
        pbuf[r] = part.astype(BF16).reshape(YL, NC, K, width)
        send(pbuf.at[r, :, 1 - c], pcore.at[r], pc_s.at[r], pc_r.at[r], at_core)
    low, high = pl.ds(0, mid), pl.ds(mid, mid)
    for r in order:
        wait_in(pcore.at[r], pc_s.at[r], pc_r.at[r])
        psum[r] = (pbuf[r, :, c].astype(F32) + pcore[r].astype(F32)).astype(BF16)
        if PZD:
            if r:
                send(psum.at[r], prz.at[r], pz_s.at[r], pz_r.at[r], at_z(r))
        elif r == 3:
            send(psum.at[r], pnear.at[0], pz_s.at[0], pz_r.at[0], at_z(1))
        elif r == 5:
            send(psum.at[r], pnear.at[1], pz_s.at[1], pz_r.at[1], at_z(Z - 1))
        elif r == 4:
            send(psum.at[r, low], pfar.at[0], pz_s.at[2], pz_r.at[2], at_z(2))
            send(psum.at[r, high], pfar.at[1], pz_s.at[3], pz_r.at[3], at_z(Z - 2))
        elif r == 1:
            send(psum.at[r], pfin.at[0], pz_s.at[4], pz_r.at[4], at_z(1))
        elif r == 7:
            send(psum.at[r], pfin.at[1], pz_s.at[5], pz_r.at[5], at_z(Z - 1))

    @(lambda f: None if WZD else pl.when((z < Z - 2))(f))
    def _():
        n = z + 2
        wait_in(wall.at[n, :, c], wz_s.at[Z - 2], wz_r.at[Z - 2])
        pass_down(n)

    @(lambda f: None if WZD else pl.when((z < 2))(f))
    def _():
        n = z + Z - 2
        wait_in(wall.at[n, :, c], wz_s.at[2], wz_r.at[2])
        pass_up(n)

    def sum_on():
        if PZD:
            return
        for e, r in enumerate((2, Z - 2)):
            wait_in(pnear.at[e], pz_s.at[e], pz_r.at[e])
            wait_in(pfar.at[e], pz_s.at[2 + e], pz_r.at[2 + e])
            total = psum[r].astype(F32) + pnear[e].astype(F32)
            for n in range(YL):
                v = total[n]
                if n // mid == e:
                    v = v + pfar[e, n % mid].astype(F32)
                pmid[e, n] = v.astype(BF16)
            send(pmid.at[e], pfin.at[2 + e], pz_s.at[6 + e], pz_r.at[6 + e], at_z(r))

    bounds = (0, 4, 6, 8)
    spans = list(zip(bounds[:-1], bounds[1:]))

    def keys(g):
        lo, hi = spans[g]
        for n in range(lo, hi):
            r = (z + Z - n) % Z
            piece = wall.at[n, :, c]
            held = (r == 0) if WZD else (r == 0) | (r == 2) | (r == Z - 2)

            @pl.when(jnp.logical_not(held) if WZD else jnp.logical_not(held) & (r != Z // 2))
            def _():
                wait_in(piece, wz_s.at[r], wz_r.at[r])

            @(lambda f: None if WZD else pl.when(r == Z // 2)(f))
            def _():
                wait_in(wall.at[n, pl.ds(0, mid), c], wz_s.at[4], wz_r.at[4])
                wait_in(wall.at[n, pl.ds(mid, mid), c], wz_s.at[0], wz_r.at[0])

            @pl.when(z != n)
            def _():
                remote(piece, piece, wc_s.at[n], wc_r.at[n], at_core).start()

        for n in range(lo, hi):
            wait_in(wall.at[n, :, 1 - c], wc_s.at[n], wc_r.at[n])
            part = lax.dot_general(
                trot[...], wall[n].reshape(group, width), (((1,), (1,)), ((), ())),
                preferred_element_type=F32,
            )
            obuf[n] = part.astype(BF16).reshape(X, YH, K, group)
        span = pl.ds(lo, hi - lo)
        ahead, behind, across = (x + 3) % X, (x + X - 3) % X, (x + X // 2) % X
        s, r = ox_s.at[g], ox_r.at[g]
        send(obuf.at[span, ahead], onear.at[0, span], s.at[0], r.at[0], at_x(1))
        send(obuf.at[span, behind], onear.at[1, span], s.at[1], r.at[1], at_x(X - 1))
        send(obuf.at[span, across, 0], ofar.at[0, span], s.at[2], r.at[2], at_x(2))
        send(obuf.at[span, across, 1], ofar.at[1, span], s.at[3], r.at[3], at_x(X - 2))
        send(obuf.at[span, (x + 1) % X], ofin.at[0, span], s.at[4], r.at[4], at_x(1))
        send(obuf.at[span, (x + X - 1) % X], ofin.at[1, span], s.at[5], r.at[5], at_x(X - 1))

    def keys_on(g):
        lo, hi = spans[g]
        span = pl.ds(lo, hi - lo)
        s, q = ox_s.at[g], ox_r.at[g]
        for e, r in enumerate((2, X - 2)):
            wait_in(onear.at[e, span], s.at[e], q.at[e])
            wait_in(ofar.at[e, span], s.at[2 + e], q.at[2 + e])
            total = obuf[lo:hi, (x + r) % X].astype(F32) + onear[e, lo:hi].astype(F32)
            for h in range(YH):
                v = total[:, h]
                if h == e:
                    v = v + ofar[e, lo:hi].astype(F32)
                omid[e, lo:hi, h] = v.astype(BF16)
            send(omid.at[e, span], ofin.at[2 + e, span], s.at[6 + e], q.at[6 + e], at_x(r))

    def keys_sum(g):
        lo, hi = spans[g]
        total = obuf[lo:hi, x].astype(F32)
        for e in range(4):
            wait_in(ofin.at[e, pl.ds(lo, hi - lo)], ox_s.at[g].at[4 + e], ox_r.at[g].at[4 + e])
            total = total + ofin[e, lo:hi].astype(F32)
        for h in range(YH):
            oy[h, lo:hi] = total[:, h].astype(BF16)
        span = pl.ds(lo, hi - lo)
        send(oy.at[1 - yh, span], ory.at[span], oy_s.at[g], oy_r.at[g], at_y(YL))

    def planes_sum():
        total = psum[0].astype(F32)
        if PZD:
            for r in range(1, Z):
                wait_in(prz.at[r], pz_s.at[r], pz_r.at[r])
                total = total + prz[r].astype(F32)
        else:
            for e in range(4):
                wait_in(pfin.at[e], pz_s.at[4 + e], pz_r.at[4 + e])
                total = total + pfin[e].astype(F32)
        py[...] = total.astype(BF16)
        for r in range(1, NY):
            send(py.at[(yl + r) % YL], pry.at[r], py_s.at[r], py_r.at[r], at_y(r))

    def rows_sum():
        total = py[yl].astype(F32) * sign(yh, yh)
        for r in range(1, NY):
            wait_in(pry.at[r], py_s.at[r], py_r.at[r])
            total = total + pry[r].astype(F32) * sign(yh, ((yy + NY - r) % NY) // YL)
        px[0] = total.astype(BF16)
        for r in range(1, X):
            send(px.at[0], px.at[r], px_s.at[r], px_r.at[r], at_x(r))

    keys(0)
    sum_on()
    keys(1)
    keys_on(0)
    keys(2)
    keys_on(1)
    planes_sum()
    keys_on(2)
    rows_sum()
    keys_sum(0)
    keys_sum(1)

    for n in range(2):
        lo, hi = n * (X // 2), (n + 1) * (X // 2)
        grad = jnp.dot(
            call[lo:hi].reshape(rows // 2, kv), wall[...].reshape(kv, width),
            preferred_element_type=F32,
        )
        grad = jnp.dot(grad.astype(BF16), signs[...], preferred_element_type=F32) * root
        gbuf[n * (rows // 2):(n + 1) * (rows // 2)] = grad.astype(BF16)
    store_g = pltpu.make_async_copy(gbuf, gtok, lsem.at[2])
    store_g.start()

    keys_sum(2)

    total = px[0].astype(F32) * sign(x, x)
    for r in range(1, X):
        wait_in(px.at[r], px_s.at[r], px_r.at[r])
        total = total + px[r].astype(F32) * sign(x, (x + X - r) % X)
    gwbuf[...] = total * F32(norm * (X * YH) ** -0.5)
    store_w = pltpu.make_async_copy(gwbuf, gwgt, lsem.at[4])
    store_w.start()

    for g, (lo, hi) in enumerate(spans):
        wait_in(ory.at[pl.ds(lo, hi - lo)], oy_s.at[g], oy_r.at[g])
    for n in range(Z):
        both = oy[yh, n].astype(F32) + ory[n].astype(F32)
        obuf_out[:, n * group:(n + 1) * group] = both.astype(BF16)
    store_o = pltpu.make_async_copy(obuf_out, out, lsem.at[3])
    store_o.start()

    for copy in sends:
        copy.wait_send()
    for n in range(Z):
        piece = wall.at[n, :, c]
        remote(piece, piece, wc_s.at[n], wc_r.at[n], at_core).wait_send()
    for e, part in () if WZD else enumerate((pl.ds(0, YL), low, pl.ds(0, YL), high)):
        piece = wall.at[z, part, c]
        remote(piece, piece, wf_s.at[e], wz_r.at[e], at_core).wait_send()
    store_g.wait()
    store_o.wait()
    store_w.wait()


def on_device(norm, tokens, weight, cotangent):
    rows, width = tokens.shape
    kv = cotangent.shape[1]
    vmem = pltpu.VMEM
    any_spec = pl.BlockSpec(memory_space=pl.ANY)
    dma = lambda n: pltpu.SemaphoreType.DMA(n if isinstance(n, tuple) else (n,))
    group = YL * NC * K
    scratch = [
        vmem((rows, width), BF16),
        vmem((rows, width), BF16),
        vmem((width, width), BF16),
        vmem((X, K, width), BF16),
        vmem((YL * YH, K, width), BF16),
        vmem((Z, YL, NC, K, width), BF16),
        vmem((X, YH, K, kv), BF16),
        vmem((Z, YL, NC, K, width), BF16),
        vmem((Z, YL, K, width), BF16),
        vmem((Z, YL, K, width), BF16),
        vmem((Z, YL, K, width), BF16),
        vmem((2, YL, K, width), BF16),
        vmem((2, YL // 2, K, width), BF16),
        vmem((2, YL, K, width), BF16),
        vmem((4, YL, K, width), BF16),
        vmem((YL, K, width), BF16),
        vmem((YL * YH, K, width), BF16),
        vmem((X, K, width), BF16),
        vmem((Z, X, YH, K, group), BF16),
        vmem((2, Z, YH, K, group), BF16),
        vmem((2, Z, K, group), BF16),
        vmem((2, Z, YH, K, group), BF16),
        vmem((4, Z, YH, K, group), BF16),
        vmem((YH, Z, K, group), BF16),
        vmem((Z, K, group), BF16),
        vmem((K, kv), BF16),
        vmem((rows, width), BF16),
        vmem((K, width), F32),
        dma(6),
    ]
    for n in (X, YL * YH, Z):
        scratch += [dma(n), dma(n)]
    scratch += [dma(4)]
    for n in (Z, 1, X, X, Z, 8, YL * YH, X, (3, 8), 3):
        scratch += [dma(n), dma(n)]
    return pl.pallas_call(
        functools.partial(kernel, norm),
        out_shape=(
            jax.ShapeDtypeStruct((K, kv), BF16),
            jax.ShapeDtypeStruct((rows, width), BF16),
            jax.ShapeDtypeStruct((K, width), F32),
        ),
        in_specs=[pl.BlockSpec(memory_space=pltpu.HBM)] * 3,
        out_specs=(any_spec,) * 3,
        scratch_shapes=scratch,
        compiler_params=pltpu.CompilerParams(
            collective_id=0, has_side_effects=True, vmem_limit_bytes=63 * 2**20
        ),
    )(tokens, weight, cotangent)


def solution(mesh):
    assert dict(mesh.shape) == {"dp": Z * YL * NC, "tensor": X * YH}

    def whole(tokens, weight, cotangent):
        return jax.shard_map(
            functools.partial(on_device, tokens.shape[0] ** -0.5),
            mesh=mesh,
            in_specs=(P("dp", "tensor"), P("dp", "tensor"), P(("dp", "tensor"), None)),
            out_specs=(P(("dp", "tensor"), None), P("dp", "tensor"), P("dp", "tensor")),
            check_vma=False,
        )(tokens, weight, cotangent)

    return whole
```
